1024 devices in a mesh: path: 64 (over z_lo, y, core), fsdp: 16 (over z_hi, x).
Axes of the slice: x: 4, y: 8, z: 16 (z_hi: 4, z_lo: 4; z = z_hi * 4 + z_lo), core: 2. Of those that a mesh axis runs over, the one named last changes fastest.
Arguments:
- cotangent: bfloat16 [64, 2048, 1024], P('path', 'fsdp'), may hold values from -6 to 6
- hidden: bfloat16 [64, 2048, 4096], P('path', 'fsdp'), may hold values from -6 to 6
- drift: bfloat16 [2, 64, 1024, 4096], P(None, 'path', None, 'fsdp'), may hold values from -6 to 6
- counts: int32 [64], replicated, may hold values from 512 to 2048, as said below
- assignment: int32 [2, 64], replicated, may hold values from 0 to 7, as said below
- outer_params: float32 [2, 8, 1024, 4096], P(None, None, 'path', 'fsdp'), may hold values from -6 to 6
- outer_moment: float32 [2, 8, 1024, 4096], P(None, None, 'path', 'fsdp'), may hold values from -3 to 3
Outputs:
- new_params: float32 [2, 8, 1024, 4096], P(None, None, 'path', 'fsdp')
- new_moment: float32 [2, 8, 1024, 4096], P(None, None, 'path', 'fsdp')
The draws below stay inside these ranges and needn't reach their ends.
Inputs may be any that keep to these rules, and one draw needn't show every extreme that they name: `counts`: some path has exactly 2048 live tokens and some exactly 512. `assignment`: at each level every module has exactly 8 paths.
All inputs are finite; a program needn't handle non-finite values.
Results may differ from the reference program's by a relative error of at most 0.0016.
Values may be sent and summed in bfloat16 or wider, within the bound.
No kernel may reach another device: no remote copies, remote signals or barrier semaphores. Data moves between devices by JAX's collectives and lax.ppermute only.
A program may use at most 32 MiB of HBM per device.

```python
import jax
import jax.numpy as jnp
from jax import lax

D_WIN = 1024
FF_WIN = 4096
MODULES = 8
TOKENS = 2048
PATHS = 64


def draw_counts(key, part):
    key = jax.random.fold_in(key, 11)
    base = jax.random.randint(jax.random.fold_in(key, 1), (PATHS,), TOKENS // 4, TOKENS + 1)
    order = jax.random.permutation(jax.random.fold_in(key, 2), PATHS)
    base = base.at[order[0]].set(TOKENS)
    base = base.at[order[1]].set(TOKENS // 4)
    return base.astype(jnp.int32)


def draw_assignment(key, part):
    key = jax.random.fold_in(key, 23)
    lower = jax.random.permutation(jax.random.fold_in(key, 1), PATHS) // (PATHS // MODULES)
    upper = jax.random.permutation(jax.random.fold_in(key, 2), PATHS) // (PATHS // MODULES)
    return jnp.stack([lower, upper]).astype(jnp.int32)


def steps_of(key, dims, cuts, least, top_value):
    def one(dim, blocks):
        steps = jax.random.uniform(jax.random.fold_in(jax.random.fold_in(key, 6), dim), (blocks,), jnp.float32, least / len(cuts), top_value / len(cuts))
        return jnp.repeat(jnp.exp(steps), dims[dim] // blocks).reshape((-1,) + (1,) * (len(dims) - dim - 1))

    loudness = one(*cuts[0])
    for cut in cuts[1:]:
        loudness = loudness * one(*cut)
    return loudness


def centred(key, shape, width, reach, cuts=(), held_as=jnp.bfloat16):
    array = jax.random.normal(key, shape, jnp.float32) * width
    if len(cuts) > 0:
        array = steps_of(key, shape, cuts, -0.22, 0.18) * array
    return jnp.clip(array, min=-reach, max=reach).astype(held_as)


def setup_inputs(seed: int = 0) -> dict:
    seeds = jax.random.split(jax.random.key(seed), 8)
    cotangent = centred(seeds[0], (PATHS, TOKENS, D_WIN), 1.0, 6.0, ((0, 64), (1, 16)))
    hidden = centred(seeds[1], (PATHS, TOKENS, FF_WIN), 1.0, 6.0, ((0, 64), (1, 16)))
    drift = centred(seeds[2], (2, PATHS, D_WIN, FF_WIN), 1.0, 6.0, ((1, 64), (3, 16)))
    counts = draw_counts(jax.random.fold_in(seeds[7], 71), 0)
    assignment = draw_assignment(jax.random.fold_in(seeds[7], 71), 0)
    outer_params = centred(seeds[5], (2, MODULES, D_WIN, FF_WIN), 1.0, 6.0, ((2, 64), (3, 16)), jnp.float32)
    outer_moment = centred(seeds[6], (2, MODULES, D_WIN, FF_WIN), 0.5, 3.0, ((2, 64), (3, 16)), jnp.float32)
    return {"cotangent": cotangent, "hidden": hidden, "drift": drift, "counts": counts, "assignment": assignment, "outer_params": outer_params, "outer_moment": outer_moment}


inner_step = 0.02
momentum_rate = 0.9
outer_rate = 0.7


def reference(cotangent, hidden, drift, counts, assignment, outer_params, outer_moment):
    positions = jnp.arange(TOKENS, dtype=jnp.int32)
    member = (assignment[:, None, :] == jnp.arange(MODULES, dtype=jnp.int32)[None, :, None]).astype(jnp.float32)
    weighted = member * counts[None, None, :].astype(jnp.float32)
    shares = weighted / jnp.sum(weighted, axis=-1, keepdims=True)

    def one_path(total, index):
        live = (positions < counts[index])[:, None]
        masked = jnp.where(live, cotangent[index], jnp.zeros((), cotangent.dtype))
        grad = lax.dot_general(masked, hidden[index], (((0,), (0,)), ((), ())), preferred_element_type=jnp.float32)
        upper = (drift[1, index].astype(jnp.float32) + inner_step * grad).astype(jnp.bfloat16)
        deltas = jnp.stack([drift[0, index], upper]).astype(jnp.float32)
        total = total + shares[:, :, index][:, :, None, None] * deltas[:, None]
        return total, None

    start = jnp.zeros((2, MODULES, D_WIN, FF_WIN), jnp.float32)
    average, _ = lax.scan(one_path, start, jnp.arange(PATHS, dtype=jnp.int32))
    new_moment = momentum_rate * outer_moment + average
    new_params = outer_params - outer_rate * (average + momentum_rate * new_moment)
    return new_params, new_moment
```

```python
import jax
import jax.numpy as jnp
from jax import lax
from jax.sharding import Mesh, PartitionSpec as P

inner_step = 0.02
momentum_rate = 0.9
outer_rate = 0.7

PATH = ("zl", "y", "core")
FSDP = ("zh", "x")
NX = 4
NZ = 4


def shift(axis, size, by):
    return [(i, (i + by) % size) for i in range(size)]


def combine(received, shares):
    return jnp.einsum(
        "mp,prc->mrc", shares, received.astype(jnp.float32), precision=lax.Precision.HIGHEST
    )


def body(cotangent, hidden, drift, counts, assignment, outer_params, outer_moment):
    path_index = lax.axis_index(PATH)
    zh = lax.axis_index("zh")
    x = lax.axis_index("x")
    paths = counts.shape[0]
    modules = outer_params.shape[1]
    owner_rows = outer_params.shape[2]
    cols = outer_params.shape[3]
    rows = cotangent.shape[1]
    width = cotangent.shape[2]
    member = (assignment[:, None, :] == jnp.arange(modules, dtype=jnp.int32)[None, :, None]).astype(
        jnp.float32
    )
    weighted = member * counts[None, None, :].astype(jnp.float32)
    shares = weighted / jnp.sum(weighted, axis=-1, keepdims=True)
    my_count = jnp.sum(jnp.where(jnp.arange(paths, dtype=jnp.int32) == path_index, counts, 0))

    got0 = lax.all_to_all(
        drift[0, 0].reshape(paths, owner_rows, cols), PATH, split_axis=0, concat_axis=0, tiled=True
    )

    positions = (zh * NX + x) * rows + jnp.arange(rows, dtype=jnp.int32)
    masked = jnp.where(
        (positions < my_count)[:, None], cotangent[0], jnp.zeros((), cotangent.dtype)
    )
    by_x = hidden[0].reshape(rows, NZ, NX, cols)

    def piece(to):
        return lax.dynamic_index_in_dim(by_x, to, 2, keepdims=False).reshape(rows, NZ * cols)

    pieces = [jnp.concatenate([masked, piece(x)], axis=1)]
    for by in (1, 2, 3):
        packed = jnp.concatenate([masked, piece((x + by) % NX)], axis=1)
        pieces.append(lax.ppermute(packed, "x", shift("x", NX, by)))
    tokens = jnp.concatenate(pieces, axis=0)
    grad = lax.dot_general(
        tokens[:, :width],
        tokens[:, width:],
        (((0,), (0,)), ((), ())),
        preferred_element_type=jnp.float32,
    )
    own = (jnp.arange(NZ) == zh)[None, :, None]
    upper = inner_step * grad.reshape(width, NZ, cols) + jnp.where(
        own, drift[1, 0].astype(jnp.float32)[:, None, :], 0.0
    )
    upper = upper.astype(jnp.bfloat16).reshape(paths, owner_rows, NZ * cols)
    got1 = lax.all_to_all(upper, PATH, split_axis=0, concat_axis=0, tiled=True)
    part1 = combine(got1, shares[1]).reshape(modules, owner_rows, NZ, cols)
    average0 = combine(got0, shares[0])
    average1 = lax.dynamic_index_in_dim(part1, zh, 2, keepdims=False)
    for by in (1, 2, 3):
        block = lax.dynamic_index_in_dim(part1, (zh + by) % NZ, 2, keepdims=False)
        average1 = average1 + lax.ppermute(
            block.astype(jnp.bfloat16), "zh", shift("zh", NZ, by)
        ).astype(jnp.float32)
    average = jnp.stack([average0, average1])
    new_moment = momentum_rate * outer_moment + average
    new_params = outer_params - outer_rate * (average + momentum_rate * new_moment)
    return (new_params, new_moment)


def solution(mesh):
    fine = Mesh(mesh.devices.reshape(4, 8, 2, 4, 4), ("zl", "y", "core", "zh", "x"))
    placed = (
        P(PATH, FSDP, None),
        P(PATH, FSDP, None),
        P(None, PATH, None, FSDP),
        P(),
        P(),
        P(None, None, PATH, FSDP),
        P(None, None, PATH, FSDP),
    )
    return jax.shard_map(
        body,
        mesh=fine,
        in_specs=placed,
        out_specs=(P(None, None, PATH, FSDP), P(None, None, PATH, FSDP)),
        check_vma=False,
    )
```

```python
import functools

import jax
import jax.numpy as jnp
from jax import lax
from jax.experimental import pallas as pl
from jax.experimental.pallas import tpu as pltpu
from jax.sharding import Mesh, PartitionSpec as P

inner_step = 0.02
momentum_rate = 0.9
outer_rate = 0.7

PATH = ("zl", "y", "core")
FSDP = ("zh", "x")
NX = 4
NZ = 4
LIMIT = 24 * 2**20
SMEM = pl.BlockSpec(memory_space=pltpu.SMEM)
VMEM = pl.BlockSpec(memory_space=pltpu.VMEM)


def shift(axis, size, by):
    return [(i, (i + by) % size) for i in range(size)]


def params():
    return pltpu.CompilerParams(vmem_limit_bytes=LIMIT)


def pack_kernel(where, cot, hid, *outs):
    width = cot.shape[2]
    cols = hid.shape[2] // (NX * NZ)
    for k, out in enumerate(outs):
        to = (where[1] + k) % NX
        out[:, :width] = cot[0]
        for j in range(NZ):
            z = (where[0] + j) % NZ
            start = pl.multiple_of((z * NX + to) * cols, cols)
            out[:, width + j * cols : width + (j + 1) * cols] = hid[0, :, pl.ds(start, cols)]


def masked_product(where, pieces, at, block, first, last):
    rows = pieces[0].shape[0]
    left = []
    for k, piece in enumerate(pieces):
        source = (where[1] - k + NX) % NX
        token = (where[0] * NX + source) * rows + lax.broadcasted_iota(jnp.int32, (rows, block), 0)
        value = piece[:, pl.ds(at, block)].astype(jnp.float32)
        left.append(jnp.where(token < where[2], value, 0.0).astype(jnp.bfloat16))
    return inner_step * lax.dot_general(
        jnp.concatenate(left, axis=0),
        jnp.concatenate([piece[:, first:last] for piece in pieces], axis=0),
        (((0,), (0,)), ((), ())),
        preferred_element_type=jnp.float32,
    )


def grad_kernel(where, *refs):
    *pieces, drift, out = refs
    block, cols = drift.shape[2:]
    at = pl.multiple_of(pl.program_id(0) * block, block)
    first = pieces[0].shape[1] - NZ * cols
    part = masked_product(where, pieces, at, block, first, first + NZ * cols)
    out[:, :cols] = (part[:, :cols] + drift[1, 0].astype(jnp.float32)).astype(out.dtype)
    out[:, cols : NZ * cols] = part[:, cols:].astype(out.dtype)
    out[:, NZ * cols :] = drift[0, 0]


def add_paths(weights, modules, level, got, at, total):
    wide = total.shape[2]

    def add(p, carry):
        m = modules[level, p]
        total[m] = total[m] + weights[level, p] * got[p, :, at : at + wide].astype(jnp.float32)
        return carry

    lax.fori_loop(0, got.shape[0], add, 0, unroll=4)


def level1_kernel(where, weights, modules, got, own, out, total):
    cols = out.shape[3]
    total[...] = jnp.zeros_like(total)
    add_paths(weights, modules, 1, got, 0, total)
    own[...] = total[:, :, :cols]
    out[where[0]] = jnp.zeros(out.shape[1:], out.dtype)
    for k in range(1, NZ):
        out[(where[0] + k) % NZ] = total[:, :, k * cols : (k + 1) * cols].astype(out.dtype)


def level0_kernel(weights, modules, got, out):
    out[...] = jnp.zeros_like(out)
    add_paths(weights, modules, 0, got, got.shape[2] - out.shape[2], out)


def update_kernel(average0, own, parts, outer_params, outer_moment, new_params, new_moment):
    for level in range(2):
        if level == 0:
            average = average0[...]
        else:
            average = functools.reduce(lambda a, b: a + b, [parts[k].astype(jnp.float32) for k in range(NZ)])
            average = average + own[...]
        moment = momentum_rate * outer_moment[level] + average
        new_moment[level] = moment
        new_params[level] = outer_params[level] - outer_rate * (average + momentum_rate * moment)


def body(cotangent, hidden, drift, counts, assignment, outer_params, outer_moment):
    path_index = lax.axis_index(PATH)
    zh = lax.axis_index("zh")
    x = lax.axis_index("x")
    paths = counts.shape[0]
    modules = outer_params.shape[1]
    owner_rows = outer_params.shape[2]
    cols = outer_params.shape[3]
    rows = cotangent.shape[1]
    width = cotangent.shape[2]
    packed_shape = (rows, width + NZ * cols)
    bf16, f32 = jnp.bfloat16, jnp.float32

    place = jnp.stack([zh, x]).astype(jnp.int32)
    packed = pl.pallas_call(
        pack_kernel,
        out_shape=[jax.ShapeDtypeStruct(packed_shape, bf16)] * NX,
        in_specs=[SMEM, VMEM, VMEM],
        out_specs=[VMEM] * NX,
        compiler_params=params(),
    )(place, cotangent, hidden)
    pieces = [packed[0]] + [lax.ppermute(packed[k], "x", shift("x", NX, k)) for k in range(1, NX)]

    member = (assignment[:, None, :] == jnp.arange(modules, dtype=jnp.int32)[None, :, None]).astype(f32)
    weighted = member * counts[None, None, :].astype(f32)
    shares = weighted / jnp.sum(weighted, axis=-1, keepdims=True)
    weights = jnp.sum(shares, axis=1)
    my_count = jnp.sum(jnp.where(jnp.arange(paths, dtype=jnp.int32) == path_index, counts, 0))
    where = jnp.stack([zh, x, my_count]).astype(jnp.int32)

    block = 256
    whole = pl.BlockSpec(packed_shape, lambda r: (0, 0))
    wide = (NZ + 1) * cols
    send = pl.pallas_call(
        grad_kernel,
        out_shape=jax.ShapeDtypeStruct((width, wide), bf16),
        grid=(width // block,),
        in_specs=[SMEM]
        + [whole] * NX
        + [pl.BlockSpec((2, 1, block, cols), lambda r: (0, 0, r, 0))],
        out_specs=pl.BlockSpec((block, wide), lambda r: (r, 0)),
        compiler_params=params(),
    )(where, *pieces, drift)
    got = lax.all_to_all(
        send.reshape(paths, owner_rows, wide), PATH, split_axis=0, concat_axis=0, tiled=True
    )
    own, sums = pl.pallas_call(
        level1_kernel,
        out_shape=[
            jax.ShapeDtypeStruct((modules, owner_rows, cols), f32),
            jax.ShapeDtypeStruct((NZ, modules, owner_rows, cols), bf16),
        ],
        in_specs=[SMEM, SMEM, SMEM, VMEM],
        out_specs=[VMEM, VMEM],
        scratch_shapes=[pltpu.VMEM((modules, owner_rows, NZ * cols), f32)],
        compiler_params=params(),
    )(place, weights, assignment, got)
    parts = lax.all_to_all(sums, "zh", split_axis=0, concat_axis=0, tiled=True)
    average0 = pl.pallas_call(
        level0_kernel,
        out_shape=jax.ShapeDtypeStruct((modules, owner_rows, cols), f32),
        in_specs=[SMEM, SMEM, VMEM],
        out_specs=VMEM,
        compiler_params=params(),
    )(weights, assignment, got)
    return pl.pallas_call(
        update_kernel,
        out_shape=[jax.ShapeDtypeStruct(outer_params.shape, f32)] * 2,
        in_specs=[VMEM] * 5,
        out_specs=[VMEM] * 2,
        compiler_params=params(),
    )(average0, own, parts, outer_params, outer_moment)


def solution(mesh):
    fine = Mesh(mesh.devices.reshape(4, 8, 2, 4, 4), ("zl", "y", "core", "zh", "x"))
    placed = (
        P(PATH, FSDP, None),
        P(PATH, FSDP, None),
        P(None, PATH, None, FSDP),
        P(),
        P(),
        P(None, None, PATH, FSDP),
        P(None, None, PATH, FSDP),
    )
    return jax.shard_map(
        lambda *a: tuple(body(*a)),
        mesh=fine,
        in_specs=placed,
        out_specs=(P(None, None, PATH, FSDP), P(None, None, PATH, FSDP)),
        check_vma=False,
    )
```

```python
import functools

import jax
import jax.numpy as jnp
from jax import lax
from jax.experimental import pallas as pl
from jax.experimental.pallas import tpu as pltpu
from jax.sharding import Mesh, PartitionSpec as P

inner_step = 0.02
momentum_rate = 0.9
outer_rate = 0.7

PATH = ("zl", "y", "core")
FSDP = ("zh", "x")
NX = 4
NZ = 4
LIMIT = 24 * 2**20
SMEM = pl.BlockSpec(memory_space=pltpu.SMEM)
VMEM = pl.BlockSpec(memory_space=pltpu.VMEM)


def shift(axis, size, by):
    return [(i, (i + by) % size) for i in range(size)]


def params():
    return pltpu.CompilerParams(vmem_limit_bytes=LIMIT)


def pack_kernel(where, cot, hid, *outs):
    width = cot.shape[2]
    cols = hid.shape[2] // (NX * NZ)
    for k, out in enumerate(outs):
        to = (where[1] + k) % NX
        out[:, :width] = cot[0]
        for j in range(NZ):
            z = (where[0] + j) % NZ
            start = pl.multiple_of((z * NX + to) * cols, cols)
            out[:, width + j * cols : width + (j + 1) * cols] = hid[0, :, pl.ds(start, cols)]


def masked_product(where, pieces, at, block, first, last):
    rows = pieces[0].shape[0]
    left = []
    for k, piece in enumerate(pieces):
        source = (where[1] - k + NX) % NX
        token = (where[0] * NX + source) * rows + lax.broadcasted_iota(jnp.int32, (rows, block), 0)
        value = piece[:, pl.ds(at, block)].astype(jnp.float32)
        left.append(jnp.where(token < where[2], value, 0.0).astype(jnp.bfloat16))
    return inner_step * lax.dot_general(
        jnp.concatenate(left, axis=0),
        jnp.concatenate([piece[:, first:last] for piece in pieces], axis=0),
        (((0,), (0,)), ((), ())),
        preferred_element_type=jnp.float32,
    )


def foreign_kernel(where, *refs):
    *pieces, out = refs
    block, wide = out.shape
    at = pl.multiple_of(pl.program_id(0) * block, block)
    last = pieces[0].shape[1]
    out[...] = masked_product(where, pieces, at, block, last - wide, last).astype(out.dtype)


def own_kernel(where, *refs):
    *pieces, drift, _, out = refs
    block, cols = drift.shape[2:]
    at = pl.multiple_of(pl.program_id(0) * block, block)
    first = pieces[0].shape[1] - NZ * cols
    part = masked_product(where, pieces, at, block, first, first + cols)
    out[:, :cols] = (part + drift[1, 0].astype(jnp.float32)).astype(out.dtype)
    out[:, cols:] = drift[0, 0]


def module_kernel(weights, modules, got, *refs):
    *outs, total = refs
    cols = outs[0].shape[2]
    total[...] = jnp.zeros_like(total)

    def add(p, carry):
        m = modules[1, p]
        total[m] = total[m] + weights[1, p] * got[p].astype(jnp.float32)
        return carry

    lax.fori_loop(0, got.shape[0], add, 0, unroll=4)
    for k, out in enumerate(outs):
        out[...] = total[:, :, k * cols : (k + 1) * cols].astype(out.dtype)


def update_kernel(weights, modules, got, *refs):
    *parts, outer_params, outer_moment, new_params, new_moment, total = refs
    cols = outer_params.shape[3]
    total[0] = jnp.zeros(total.shape[1:], jnp.float32)
    total[1] = functools.reduce(lambda a, b: a + b, [part[...].astype(jnp.float32) for part in parts])

    def add(p, carry):
        for level in range(2):
            m = modules[level, p]
            value = got[p, :, (1 - level) * cols : (2 - level) * cols].astype(jnp.float32)
            total[level, m] = total[level, m] + weights[level, p] * value
        return carry

    lax.fori_loop(0, got.shape[0], add, 0, unroll=4)
    for level in range(2):
        average = total[level]
        moment = momentum_rate * outer_moment[level] + average
        new_moment[level] = moment
        new_params[level] = outer_params[level] - outer_rate * (average + momentum_rate * moment)


def body(cotangent, hidden, drift, counts, assignment, outer_params, outer_moment):
    path_index = lax.axis_index(PATH)
    zh = lax.axis_index("zh")
    x = lax.axis_index("x")
    paths = counts.shape[0]
    modules = outer_params.shape[1]
    owner_rows = outer_params.shape[2]
    cols = outer_params.shape[3]
    rows = cotangent.shape[1]
    width = cotangent.shape[2]
    packed_shape = (rows, width + NZ * cols)
    foreign_cols = (NZ - 1) * cols
    bf16, f32 = jnp.bfloat16, jnp.float32

    place = jnp.stack([zh, x]).astype(jnp.int32)
    packed = pl.pallas_call(
        pack_kernel,
        out_shape=[jax.ShapeDtypeStruct(packed_shape, bf16)] * NX,
        in_specs=[SMEM, VMEM, VMEM],
        out_specs=[VMEM] * NX,
        compiler_params=params(),
    )(place, cotangent, hidden)
    pieces = [packed[0]] + [lax.ppermute(packed[k], "x", shift("x", NX, k)) for k in range(1, NX)]

    member = (assignment[:, None, :] == jnp.arange(modules, dtype=jnp.int32)[None, :, None]).astype(f32)
    weighted = member * counts[None, None, :].astype(f32)
    shares = weighted / jnp.sum(weighted, axis=-1, keepdims=True)
    weights = jnp.sum(shares, axis=1)
    my_count = jnp.sum(jnp.where(jnp.arange(paths, dtype=jnp.int32) == path_index, counts, 0))
    where = jnp.stack([zh, x, my_count]).astype(jnp.int32)

    block = 256
    whole = pl.BlockSpec(packed_shape, lambda r: (0, 0))
    foreign = pl.pallas_call(
        foreign_kernel,
        out_shape=jax.ShapeDtypeStruct((width, foreign_cols), bf16),
        grid=(width // block,),
        in_specs=[SMEM] + [whole] * NX,
        out_specs=pl.BlockSpec((block, foreign_cols), lambda r: (r, 0)),
        compiler_params=params(),
    )(where, *pieces)
    got_foreign = lax.all_to_all(
        foreign.reshape(paths, owner_rows, foreign_cols), PATH, split_axis=0, concat_axis=0, tiled=True
    )
    own = pl.pallas_call(
        own_kernel,
        out_shape=jax.ShapeDtypeStruct((width, 2 * cols), bf16),
        grid=(width // block,),
        in_specs=[SMEM]
        + [whole] * NX
        + [pl.BlockSpec((2, 1, block, cols), lambda r: (0, 0, r, 0)), pl.BlockSpec(memory_space=pl.ANY)],
        out_specs=pl.BlockSpec((block, 2 * cols), lambda r: (r, 0)),
        compiler_params=params(),
    )(where, *pieces, drift, foreign)
    got_own = lax.all_to_all(
        own.reshape(paths, owner_rows, 2 * cols), PATH, split_axis=0, concat_axis=0, tiled=True
    )
    sums = pl.pallas_call(
        module_kernel,
        out_shape=[jax.ShapeDtypeStruct((modules, owner_rows, cols), bf16)] * (NZ - 1),
        in_specs=[SMEM, SMEM, VMEM],
        out_specs=[VMEM] * (NZ - 1),
        scratch_shapes=[pltpu.VMEM((modules, owner_rows, foreign_cols), f32)],
        compiler_params=params(),
    )(weights, assignment, got_foreign)
    parts = [lax.ppermute(sums[k - 1], "zh", shift("zh", NZ, k)) for k in range(1, NZ)]
    return pl.pallas_call(
        update_kernel,
        out_shape=[jax.ShapeDtypeStruct(outer_params.shape, f32)] * 2,
        in_specs=[SMEM, SMEM] + [VMEM] * (NZ + 2),
        out_specs=[VMEM] * 2,
        scratch_shapes=[pltpu.VMEM((2, modules, owner_rows, cols), f32)],
        compiler_params=params(),
    )(weights, assignment, got_own, *parts, outer_params, outer_moment)


def solution(mesh):
    fine = Mesh(mesh.devices.reshape(4, 8, 2, 4, 4), ("zl", "y", "core", "zh", "x"))
    placed = (
        P(PATH, FSDP, None),
        P(PATH, FSDP, None),
        P(None, PATH, None, FSDP),
        P(),
        P(),
        P(None, None, PATH, FSDP),
        P(None, None, PATH, FSDP),
    )
    return jax.shard_map(
        lambda *a: tuple(body(*a)),
        mesh=fine,
        in_specs=placed,
        out_specs=(P(None, None, PATH, FSDP), P(None, None, PATH, FSDP)),
        check_vma=False,
    )
```

```python
import functools

import jax
import jax.numpy as jnp
from jax import lax
from jax.experimental import pallas as pl
from jax.experimental.pallas import tpu as pltpu
from jax.sharding import Mesh, PartitionSpec as P

inner_step = 0.02
momentum_rate = 0.9
outer_rate = 0.7

PATH = ("zl", "y", "core")
FSDP = ("zh", "x")
NX = 4
NZ = 4
LIMIT = 24 * 2**20
SMEM = pl.BlockSpec(memory_space=pltpu.SMEM)
VMEM = pl.BlockSpec(memory_space=pltpu.VMEM)


def shift(axis, size, by):
    return [(i, (i + by) % size) for i in range(size)]


def params():
    return pltpu.CompilerParams(vmem_limit_bytes=LIMIT)


def pack_kernel(where, cot, hid, *outs):
    width = cot.shape[2]
    cols = hid.shape[2] // (NX * NZ)
    for k, out in enumerate(outs):
        to = (where[1] + k) % NX
        out[:, :width] = cot[0]
        for j in range(NZ):
            z = (where[0] + j) % NZ
            start = pl.multiple_of((z * NX + to) * cols, cols)
            out[:, width + j * cols : width + (j + 1) * cols] = hid[0, :, pl.ds(start, cols)]


def masked_product(where, pieces, at, block, first, last):
    rows = pieces[0].shape[0]
    left = []
    for k, piece in enumerate(pieces):
        source = (where[1] - k + NX) % NX
        token = (where[0] * NX + source) * rows + lax.broadcasted_iota(jnp.int32, (rows, block), 0)
        value = piece[:, pl.ds(at, block)].astype(jnp.float32)
        left.append(jnp.where(token < where[2], value, 0.0).astype(jnp.bfloat16))
    return inner_step * lax.dot_general(
        jnp.concatenate(left, axis=0),
        jnp.concatenate([piece[:, first:last] for piece in pieces], axis=0),
        (((0,), (0,)), ((), ())),
        preferred_element_type=jnp.float32,
    )


def foreign_kernel(where, *refs):
    *pieces, out = refs
    block, wide = out.shape
    at = pl.multiple_of(pl.program_id(0) * block, block)
    last = pieces[0].shape[1]
    out[...] = masked_product(where, pieces, at, block, last - wide, last).astype(out.dtype)


def own_kernel(where, *refs):
    *pieces, drift, _, out = refs
    block, cols = out.shape
    at = pl.multiple_of(pl.program_id(0) * block, block)
    first = pieces[0].shape[1] - NZ * cols
    part = masked_product(where, pieces, at, block, first, first + cols)
    out[...] = (part + drift[0, 0].astype(jnp.float32)).astype(out.dtype)


def copy_kernel(source, _, out):
    out[...] = source[0, 0]


def module_kernel(weights, modules, got, *refs):
    *outs, total = refs
    cols = outs[0].shape[2]
    total[...] = jnp.zeros_like(total)

    def add(p, carry):
        m = modules[1, p]
        total[m] = total[m] + weights[1, p] * got[p].astype(jnp.float32)
        return carry

    lax.fori_loop(0, got.shape[0], add, 0, unroll=4)
    for k, out in enumerate(outs):
        out[...] = total[:, :, k * cols : (k + 1) * cols].astype(out.dtype)


def update_kernel(weights, modules, got0, got1, *refs):
    *parts, outer_params, outer_moment, new_params, new_moment, total = refs
    total[0] = jnp.zeros(total.shape[1:], jnp.float32)
    total[1] = functools.reduce(lambda a, b: a + b, [part[...].astype(jnp.float32) for part in parts])

    def add(p, carry):
        for level, got in ((0, got0), (1, got1)):
            m = modules[level, p]
            total[level, m] = total[level, m] + weights[level, p] * got[p].astype(jnp.float32)
        return carry

    lax.fori_loop(0, got0.shape[0], add, 0, unroll=4)
    for level in range(2):
        average = total[level]
        moment = momentum_rate * outer_moment[level] + average
        new_moment[level] = moment
        new_params[level] = outer_params[level] - outer_rate * (average + momentum_rate * moment)


def body(cotangent, hidden, drift, counts, assignment, outer_params, outer_moment):
    path_index = lax.axis_index(PATH)
    zh = lax.axis_index("zh")
    x = lax.axis_index("x")
    paths = counts.shape[0]
    modules = outer_params.shape[1]
    owner_rows = outer_params.shape[2]
    cols = outer_params.shape[3]
    rows = cotangent.shape[1]
    width = cotangent.shape[2]
    packed_shape = (rows, width + NZ * cols)
    foreign_cols = (NZ - 1) * cols
    bf16, f32 = jnp.bfloat16, jnp.float32

    place = jnp.stack([zh, x]).astype(jnp.int32)
    packed = pl.pallas_call(
        pack_kernel,
        out_shape=[jax.ShapeDtypeStruct(packed_shape, bf16)] * NX,
        in_specs=[SMEM, VMEM, VMEM],
        out_specs=[VMEM] * NX,
        compiler_params=params(),
    )(place, cotangent, hidden)
    pieces = [packed[0]] + [lax.ppermute(packed[k], "x", shift("x", NX, k)) for k in range(1, NX)]

    send0 = pl.pallas_call(
        copy_kernel,
        out_shape=jax.ShapeDtypeStruct((width, cols), bf16),
        grid=(1,),
        in_specs=[
            pl.BlockSpec((1, 1, width, cols), lambda r: (0, 0, 0, 0)),
            pl.BlockSpec(memory_space=pl.ANY),
        ],
        out_specs=pl.BlockSpec((width, cols), lambda r: (0, 0)),
        compiler_params=params(),
    )(drift, packed[1])
    got0 = lax.all_to_all(
        send0.reshape(paths, owner_rows, cols), PATH, split_axis=0, concat_axis=0, tiled=True
    )

    member = (assignment[:, None, :] == jnp.arange(modules, dtype=jnp.int32)[None, :, None]).astype(f32)
    weighted = member * counts[None, None, :].astype(f32)
    shares = weighted / jnp.sum(weighted, axis=-1, keepdims=True)
    weights = jnp.sum(shares, axis=1)
    my_count = jnp.sum(jnp.where(jnp.arange(paths, dtype=jnp.int32) == path_index, counts, 0))
    where = jnp.stack([zh, x, my_count]).astype(jnp.int32)

    block = 256
    whole = pl.BlockSpec(packed_shape, lambda r: (0, 0))
    foreign = pl.pallas_call(
        foreign_kernel,
        out_shape=jax.ShapeDtypeStruct((width, foreign_cols), bf16),
        grid=(width // block,),
        in_specs=[SMEM] + [whole] * NX,
        out_specs=pl.BlockSpec((block, foreign_cols), lambda r: (r, 0)),
        compiler_params=params(),
        cost_estimate=pl.CostEstimate(flops=30 * 10**9, bytes_accessed=4 * 10**6, transcendentals=0),
    )(where, *pieces)
    foreign, got0 = lax.optimization_barrier((foreign, got0))
    got_foreign = lax.all_to_all(
        foreign.reshape(paths, owner_rows, foreign_cols), PATH, split_axis=0, concat_axis=0, tiled=True
    )
    own = pl.pallas_call(
        own_kernel,
        out_shape=jax.ShapeDtypeStruct((width, cols), bf16),
        grid=(width // block,),
        in_specs=[SMEM]
        + [whole] * NX
        + [pl.BlockSpec((1, 1, block, cols), lambda r: (1, 0, r, 0)), pl.BlockSpec(memory_space=pl.ANY)],
        out_specs=pl.BlockSpec((block, cols), lambda r: (r, 0)),
        compiler_params=params(),
    )(where, *pieces, drift, foreign)
    got_own = lax.all_to_all(
        own.reshape(paths, owner_rows, cols), PATH, split_axis=0, concat_axis=0, tiled=True
    )
    sums = pl.pallas_call(
        module_kernel,
        out_shape=[jax.ShapeDtypeStruct((modules, owner_rows, cols), bf16)] * (NZ - 1),
        in_specs=[SMEM, SMEM, VMEM],
        out_specs=[VMEM] * (NZ - 1),
        scratch_shapes=[pltpu.VMEM((modules, owner_rows, foreign_cols), f32)],
        compiler_params=params(),
    )(weights, assignment, got_foreign)
    parts = [lax.ppermute(sums[k - 1], "zh", shift("zh", NZ, k)) for k in range(1, NZ)]
    return pl.pallas_call(
        update_kernel,
        out_shape=[jax.ShapeDtypeStruct(outer_params.shape, f32)] * 2,
        in_specs=[SMEM, SMEM] + [VMEM] * (NZ + 3),
        out_specs=[VMEM] * 2,
        scratch_shapes=[pltpu.VMEM((2, modules, owner_rows, cols), f32)],
        compiler_params=params(),
    )(weights, assignment, got0, got_own, *parts, outer_params, outer_moment)


def solution(mesh):
    fine = Mesh(mesh.devices.reshape(4, 8, 2, 4, 4), ("zl", "y", "core", "zh", "x"))
    placed = (
        P(PATH, FSDP, None),
        P(PATH, FSDP, None),
        P(None, PATH, None, FSDP),
        P(),
        P(),
        P(None, None, PATH, FSDP),
        P(None, None, PATH, FSDP),
    )
    return jax.shard_map(
        lambda *a: tuple(body(*a)),
        mesh=fine,
        in_specs=placed,
        out_specs=(P(None, None, PATH, FSDP), P(None, None, PATH, FSDP)),
        check_vma=False,
    )
```

```python
import functools

import jax
import jax.numpy as jnp
from jax import lax
from jax.experimental import pallas as pl
from jax.experimental.pallas import tpu as pltpu
from jax.sharding import Mesh, PartitionSpec as P

inner_step = 0.02
momentum_rate = 0.9
outer_rate = 0.7

PATH = ("zl", "y", "core")
FSDP = ("zh", "x")
NX = 4
NZ = 4
LIMIT = 24 * 2**20
LARGE = 56 * 2**20
SMEM = pl.BlockSpec(memory_space=pltpu.SMEM)
VMEM = pl.BlockSpec(memory_space=pltpu.VMEM)
HBM = pl.BlockSpec(memory_space=pltpu.HBM)


def shift(axis, size, by):
    return [(i, (i + by) % size) for i in range(size)]


def params(limit=LIMIT):
    return pltpu.CompilerParams(vmem_limit_bytes=limit)


def pieces_to(where, shift_x, cot, hid, out):
    width = cot.shape[2]
    cols = hid.shape[2] // (NX * NZ)
    to = (where[1] + shift_x) % NX
    pairs = [(cot.at[0], out.at[:, pl.ds(0, width)])]
    for j in range(NZ):
        z = (where[0] + j) % NZ
        start = pl.multiple_of((z * NX + to) * cols, cols)
        pairs.append((hid.at[0, :, pl.ds(start, cols)], out.at[:, pl.ds(width + j * cols, cols)]))
    return pairs


def copy_all(pairs, sems):
    copies = [pltpu.make_async_copy(a, b, sems.at[i]) for i, (a, b) in enumerate(pairs)]
    for copy in copies:
        copy.start()
    for copy in copies:
        copy.wait()


def pack_kernel(where, cot, hid, *refs):
    *outs, sems = refs
    copy_all([pair for k, out in enumerate(outs) for pair in pieces_to(where, k + 1, cot, hid, out)], sems)


def local_kernel(where, cot, hid, drift, _, own, send0, sems):
    copy_all(pieces_to(where, 0, cot, hid, own) + [(drift.at[0, 0], send0)], sems)


def masked_product(where, pieces, at, block, first, last):
    rows = pieces[0].shape[0]
    left = []
    for k, piece in enumerate(pieces):
        source = (where[1] - k + NX) % NX
        token = (where[0] * NX + source) * rows + lax.broadcasted_iota(jnp.int32, (rows, block), 0)
        value = piece[:, pl.ds(at, block)].astype(jnp.float32)
        left.append(jnp.where(token < where[2], value, 0.0).astype(jnp.bfloat16))
    return inner_step * lax.dot_general(
        jnp.concatenate(left, axis=0),
        jnp.concatenate([piece[:, first:last] for piece in pieces], axis=0),
        (((0,), (0,)), ((), ())),
        preferred_element_type=jnp.float32,
    )


def grad_kernel(where, *refs):
    *pieces, drift, foreign, own = refs
    block, cols = own.shape
    at = pl.multiple_of(pl.program_id(0) * block, block)
    last = pieces[0].shape[1]
    part = masked_product(where, pieces, at, block, last - NZ * cols, last)
    own[...] = (part[:, :cols] + drift[0, 0].astype(jnp.float32)).astype(own.dtype)
    foreign[...] = part[:, cols:].astype(foreign.dtype)


def add_paths(weights, modules, level, got, total):
    def add(p, carry):
        m = modules[level, p]
        total[m] = total[m] + weights[level, p] * got[p].astype(jnp.float32)
        return carry

    lax.fori_loop(0, got.shape[0], add, 0, unroll=4)


def module_kernel(weights, modules, got, *refs):
    *outs, total = refs
    cols = outs[0].shape[2]
    total[...] = jnp.zeros_like(total)
    add_paths(weights, modules, 1, got, total)
    for k, out in enumerate(outs):
        out[...] = total[:, :, k * cols : (k + 1) * cols].astype(out.dtype)


def level0_kernel(weights, modules, got, out):
    out[...] = jnp.zeros_like(out)
    add_paths(weights, modules, 0, got, out)


def update_kernel(weights, modules, average0, got, *refs):
    *parts, outer_params, outer_moment, new_params, new_moment, total = refs
    total[...] = functools.reduce(lambda a, b: a + b, [part[...].astype(jnp.float32) for part in parts])
    add_paths(weights, modules, 1, got, total)
    for level, average in ((0, average0[...]), (1, total[...])):
        moment = momentum_rate * outer_moment[level] + average
        new_moment[level] = moment
        new_params[level] = outer_params[level] - outer_rate * (average + momentum_rate * moment)


def body(cotangent, hidden, drift, counts, assignment, outer_params, outer_moment):
    path_index = lax.axis_index(PATH)
    zh = lax.axis_index("zh")
    x = lax.axis_index("x")
    paths = counts.shape[0]
    modules = outer_params.shape[1]
    owner_rows = outer_params.shape[2]
    cols = outer_params.shape[3]
    rows = cotangent.shape[1]
    width = cotangent.shape[2]
    packed_shape = (rows, width + NZ * cols)
    foreign_cols = (NZ - 1) * cols
    bf16, f32 = jnp.bfloat16, jnp.float32

    place = jnp.stack([zh, x]).astype(jnp.int32)
    packed = pl.pallas_call(
        pack_kernel,
        out_shape=[jax.ShapeDtypeStruct(packed_shape, bf16)] * (NX - 1),
        in_specs=[SMEM, HBM, HBM],
        out_specs=[HBM] * (NX - 1),
        scratch_shapes=[pltpu.SemaphoreType.DMA(((NX - 1) * (1 + NZ),))],
        compiler_params=params(LARGE),
    )(place, cotangent, hidden)
    pieces = [lax.ppermute(packed[k - 1], "x", shift("x", NX, k)) for k in range(1, NX)]
    piece0, send0 = pl.pallas_call(
        local_kernel,
        out_shape=[jax.ShapeDtypeStruct(packed_shape, bf16), jax.ShapeDtypeStruct((width, cols), bf16)],
        in_specs=[SMEM, HBM, HBM, HBM, HBM],
        out_specs=[HBM, HBM],
        scratch_shapes=[pltpu.SemaphoreType.DMA((2 + NZ,))],
        compiler_params=params(LARGE),
    )(place, cotangent, hidden, drift, packed[0])
    pieces = [piece0] + pieces
    got0 = lax.all_to_all(
        send0.reshape(paths, owner_rows, cols), PATH, split_axis=0, concat_axis=0, tiled=True
    )

    member = (assignment[:, None, :] == jnp.arange(modules, dtype=jnp.int32)[None, :, None]).astype(f32)
    weighted = member * counts[None, None, :].astype(f32)
    shares = weighted / jnp.sum(weighted, axis=-1, keepdims=True)
    weights = jnp.sum(shares, axis=1)
    my_count = jnp.sum(jnp.where(jnp.arange(paths, dtype=jnp.int32) == path_index, counts, 0))
    where = jnp.stack([zh, x, my_count]).astype(jnp.int32)

    block = 256
    foreign, own = pl.pallas_call(
        grad_kernel,
        out_shape=[
            jax.ShapeDtypeStruct((width, foreign_cols), bf16),
            jax.ShapeDtypeStruct((width, cols), bf16),
        ],
        grid=(width // block,),
        in_specs=[SMEM] + [VMEM] * NX + [pl.BlockSpec((1, 1, block, cols), lambda r: (1, 0, r, 0))],
        out_specs=[
            pl.BlockSpec((block, foreign_cols), lambda r: (r, 0)),
            pl.BlockSpec((block, cols), lambda r: (r, 0)),
        ],
        compiler_params=params(),
        cost_estimate=pl.CostEstimate(flops=30 * 10**9, bytes_accessed=4 * 10**6, transcendentals=0),
    )(where, *pieces, drift)
    foreign, got0 = lax.optimization_barrier((foreign, got0))
    got_foreign = lax.all_to_all(
        foreign.reshape(paths, owner_rows, foreign_cols), PATH, split_axis=0, concat_axis=0, tiled=True
    )
    got_own = lax.all_to_all(
        own.reshape(paths, owner_rows, cols), PATH, split_axis=0, concat_axis=0, tiled=True
    )
    sums = pl.pallas_call(
        module_kernel,
        out_shape=[jax.ShapeDtypeStruct((modules, owner_rows, cols), bf16)] * (NZ - 1),
        in_specs=[SMEM, SMEM, VMEM],
        out_specs=[VMEM] * (NZ - 1),
        scratch_shapes=[pltpu.VMEM((modules, owner_rows, foreign_cols), f32)],
        compiler_params=params(),
    )(weights, assignment, got_foreign)
    parts = [lax.ppermute(sums[k - 1], "zh", shift("zh", NZ, k)) for k in range(1, NZ)]
    average0 = pl.pallas_call(
        level0_kernel,
        out_shape=jax.ShapeDtypeStruct((modules, owner_rows, cols), f32),
        in_specs=[SMEM, SMEM, VMEM],
        out_specs=VMEM,
        compiler_params=params(),
    )(weights, assignment, got0)
    return pl.pallas_call(
        update_kernel,
        out_shape=[jax.ShapeDtypeStruct(outer_params.shape, f32)] * 2,
        in_specs=[SMEM, SMEM] + [VMEM] * (NZ + 3),
        out_specs=[VMEM] * 2,
        scratch_shapes=[pltpu.VMEM((modules, owner_rows, cols), f32)],
        compiler_params=params(),
    )(weights, assignment, average0, got_own, *parts, outer_params, outer_moment)


def solution(mesh):
    fine = Mesh(mesh.devices.reshape(4, 8, 2, 4, 4), ("zl", "y", "core", "zh", "x"))
    placed = (
        P(PATH, FSDP, None),
        P(PATH, FSDP, None),
        P(None, PATH, None, FSDP),
        P(),
        P(),
        P(None, None, PATH, FSDP),
        P(None, None, PATH, FSDP),
    )
    return jax.shard_map(
        lambda *a: tuple(body(*a)),
        mesh=fine,
        in_specs=placed,
        out_specs=(P(None, None, PATH, FSDP), P(None, None, PATH, FSDP)),
        check_vma=False,
    )
```

```python
import functools

import jax
import jax.numpy as jnp
from jax import lax
from jax.experimental import pallas as pl
from jax.experimental.pallas import tpu as pltpu
from jax.sharding import Mesh, PartitionSpec as P

inner_step = 0.02
momentum_rate = 0.9
outer_rate = 0.7

CHIPS = ("zl", "y")
PATH = ("zl", "y", "core")
FSDP = ("zh", "x")
NX = 4
NZ = 4
LIMIT = 24 * 2**20
LARGE = 56 * 2**20
SMEM = pl.BlockSpec(memory_space=pltpu.SMEM)
VMEM = pl.BlockSpec(memory_space=pltpu.VMEM)
HBM = pl.BlockSpec(memory_space=pltpu.HBM)


def shift(axis, size, by):
    return [(i, (i + by) % size) for i in range(size)]


def params(limit=LIMIT):
    return pltpu.CompilerParams(vmem_limit_bytes=limit)


def pieces_to(where, shift_x, cot, hid, out):
    width = cot.shape[2]
    cols = hid.shape[2] // (NX * NZ)
    to = (where[1] + shift_x) % NX
    pairs = [(cot.at[0], out.at[:, pl.ds(0, width)])]
    for j in range(NZ):
        z = (where[0] + j) % NZ
        start = pl.multiple_of((z * NX + to) * cols, cols)
        pairs.append((hid.at[0, :, pl.ds(start, cols)], out.at[:, pl.ds(width + j * cols, cols)]))
    return pairs


def copy_all(pairs, sems):
    copies = [pltpu.make_async_copy(a, b, sems.at[i]) for i, (a, b) in enumerate(pairs)]
    for copy in copies:
        copy.start()
    for copy in copies:
        copy.wait()


def pack_kernel(where, cot, hid, *refs):
    *outs, sems = refs
    copy_all([pair for k, out in enumerate(outs) for pair in pieces_to(where, k + 1, cot, hid, out)], sems)


def local_kernel(where, cot, hid, _, own, sems):
    copy_all(pieces_to(where, 0, cot, hid, own), sems)


def copy_kernel(source, _, out):
    out[...] = source[0, 0]


def masked_product(where, pieces, at, block, first, last):
    rows = pieces[0].shape[0]
    left = []
    for k, piece in enumerate(pieces):
        source = (where[1] - k + NX) % NX
        token = (where[0] * NX + source) * rows + lax.broadcasted_iota(jnp.int32, (rows, block), 0)
        value = piece[:, pl.ds(at, block)].astype(jnp.float32)
        left.append(jnp.where(token < where[2], value, 0.0).astype(jnp.bfloat16))
    return inner_step * lax.dot_general(
        jnp.concatenate(left, axis=0),
        jnp.concatenate([piece[:, first:last] for piece in pieces], axis=0),
        (((0,), (0,)), ((), ())),
        preferred_element_type=jnp.float32,
    )


def grad_kernel(where, *refs):
    *pieces, drift, foreign, own = refs
    block, cols = own.shape
    at = pl.multiple_of(pl.program_id(0) * block, block)
    last = pieces[0].shape[1]
    part = masked_product(where, pieces, at, block, last - NZ * cols, last)
    own[...] = (part[:, :cols] + drift[0, 0].astype(jnp.float32)).astype(own.dtype)
    foreign[...] = part[:, cols:].astype(foreign.dtype)


def add_paths(weights, modules, level, got, total):
    def add(p, carry):
        m = modules[level, p]
        total[m] = total[m] + weights[level, p] * got[p].astype(jnp.float32)
        return carry

    lax.fori_loop(0, got.shape[0], add, 0, unroll=4)


def module_kernel(weights, modules, got, *refs):
    *outs, total = refs
    cols = outs[0].shape[2]
    total[...] = jnp.zeros_like(total)
    add_paths(weights, modules, 1, got, total)
    for k, out in enumerate(outs):
        out[...] = total[:, :, k * cols : (k + 1) * cols].astype(out.dtype)


def level0_kernel(where, weights, modules, got, mine, other, total):
    core, rows = where[2], mine.shape[1]
    total[...] = jnp.zeros_like(total)

    def add(i, carry):
        p = 2 * i + core
        m = modules[0, p]
        total[m] = total[m] + weights[0, p] * got[i].astype(jnp.float32)
        return carry

    lax.fori_loop(0, got.shape[0], add, 0, unroll=4)
    mine[...] = total[:, pl.ds(pl.multiple_of(core * rows, rows), rows)]
    other[...] = total[:, pl.ds(pl.multiple_of((1 - core) * rows, rows), rows)]


def update_kernel(weights, modules, mine0, other0, got, *refs):
    *parts, outer_params, outer_moment, new_params, new_moment, total = refs
    total[...] = functools.reduce(lambda a, b: a + b, [part[...].astype(jnp.float32) for part in parts])
    add_paths(weights, modules, 1, got, total)
    for level, average in ((0, mine0[...] + other0[...]), (1, total[...])):
        moment = momentum_rate * outer_moment[level] + average
        new_moment[level] = moment
        new_params[level] = outer_params[level] - outer_rate * (average + momentum_rate * moment)


def body(cotangent, hidden, drift, counts, assignment, outer_params, outer_moment):
    path_index = lax.axis_index(PATH)
    zh = lax.axis_index("zh")
    x = lax.axis_index("x")
    paths = counts.shape[0]
    modules = outer_params.shape[1]
    owner_rows = outer_params.shape[2]
    cols = outer_params.shape[3]
    rows = cotangent.shape[1]
    width = cotangent.shape[2]
    packed_shape = (rows, width + NZ * cols)
    foreign_cols = (NZ - 1) * cols
    bf16, f32 = jnp.bfloat16, jnp.float32

    place = jnp.stack([zh, x, lax.axis_index("core")]).astype(jnp.int32)
    packed = pl.pallas_call(
        pack_kernel,
        out_shape=[jax.ShapeDtypeStruct(packed_shape, bf16)] * (NX - 1),
        in_specs=[SMEM, HBM, HBM],
        out_specs=[VMEM] * (NX - 1),
        scratch_shapes=[pltpu.SemaphoreType.DMA(((NX - 1) * (1 + NZ),))],
        compiler_params=params(LARGE),
    )(place, cotangent, hidden)
    pieces = [lax.ppermute(packed[k - 1], "x", shift("x", NX, k)) for k in range(1, NX)]
    send0 = pl.pallas_call(
        copy_kernel,
        out_shape=jax.ShapeDtypeStruct((width, cols), bf16),
        grid=(1,),
        in_specs=[pl.BlockSpec((1, 1, width, cols), lambda r: (0, 0, 0, 0)), HBM],
        out_specs=pl.BlockSpec((width, cols), lambda r: (0, 0)),
        compiler_params=params(LARGE),
    )(drift, packed[0])
    piece0 = pl.pallas_call(
        local_kernel,
        out_shape=jax.ShapeDtypeStruct(packed_shape, bf16),
        in_specs=[SMEM, HBM, HBM, HBM],
        out_specs=VMEM,
        scratch_shapes=[pltpu.SemaphoreType.DMA((1 + NZ,))],
        compiler_params=params(LARGE),
    )(place, cotangent, hidden, send0)
    pieces = [piece0] + pieces
    chips = paths // 2
    got0 = lax.all_to_all(
        send0.reshape(chips, 2 * owner_rows, cols), CHIPS, split_axis=0, concat_axis=0, tiled=True
    )

    member = (assignment[:, None, :] == jnp.arange(modules, dtype=jnp.int32)[None, :, None]).astype(f32)
    weighted = member * counts[None, None, :].astype(f32)
    shares = weighted / jnp.sum(weighted, axis=-1, keepdims=True)
    weights = jnp.sum(shares, axis=1)
    my_count = jnp.sum(jnp.where(jnp.arange(paths, dtype=jnp.int32) == path_index, counts, 0))
    where = jnp.stack([zh, x, my_count]).astype(jnp.int32)

    block = 256
    foreign, own = pl.pallas_call(
        grad_kernel,
        out_shape=[
            jax.ShapeDtypeStruct((width, foreign_cols), bf16),
            jax.ShapeDtypeStruct((width, cols), bf16),
        ],
        grid=(width // block,),
        in_specs=[SMEM] + [VMEM] * NX + [pl.BlockSpec((1, 1, block, cols), lambda r: (1, 0, r, 0))],
        out_specs=[
            pl.BlockSpec((block, foreign_cols), lambda r: (r, 0)),
            pl.BlockSpec((block, cols), lambda r: (r, 0)),
        ],
        compiler_params=params(),
        cost_estimate=pl.CostEstimate(flops=30 * 10**9, bytes_accessed=4 * 10**6, transcendentals=0),
    )(where, *pieces, drift)
    foreign, got0 = lax.optimization_barrier((foreign, got0))
    got_foreign = lax.all_to_all(
        foreign.reshape(paths, owner_rows, foreign_cols), PATH, split_axis=0, concat_axis=0, tiled=True
    )
    mine0, other0 = pl.pallas_call(
        level0_kernel,
        out_shape=[jax.ShapeDtypeStruct((modules, owner_rows, cols), f32)] * 2,
        in_specs=[SMEM, SMEM, SMEM, VMEM],
        out_specs=[VMEM, VMEM],
        scratch_shapes=[pltpu.VMEM((modules, 2 * owner_rows, cols), f32)],
        compiler_params=params(),
    )(place, weights, assignment, got0)
    other0 = lax.ppermute(other0, "core", shift("core", 2, 1))
    own, other0 = lax.optimization_barrier((own, other0))
    got_own = lax.all_to_all(
        own.reshape(paths, owner_rows, cols), PATH, split_axis=0, concat_axis=0, tiled=True
    )
    sums = pl.pallas_call(
        module_kernel,
        out_shape=[jax.ShapeDtypeStruct((modules, owner_rows, cols), bf16)] * (NZ - 1),
        in_specs=[SMEM, SMEM, VMEM],
        out_specs=[VMEM] * (NZ - 1),
        scratch_shapes=[pltpu.VMEM((modules, owner_rows, foreign_cols), f32)],
        compiler_params=params(),
    )(weights, assignment, got_foreign)
    parts = [lax.ppermute(sums[k - 1], "zh", shift("zh", NZ, k)) for k in range(1, NZ)]
    return pl.pallas_call(
        update_kernel,
        out_shape=[jax.ShapeDtypeStruct(outer_params.shape, f32)] * 2,
        in_specs=[SMEM, SMEM] + [VMEM] * (NZ + 4),
        out_specs=[VMEM] * 2,
        scratch_shapes=[pltpu.VMEM((modules, owner_rows, cols), f32)],
        compiler_params=params(),
    )(weights, assignment, mine0, other0, got_own, *parts, outer_params, outer_moment)


def solution(mesh):
    fine = Mesh(mesh.devices.reshape(4, 8, 2, 4, 4), ("zl", "y", "core", "zh", "x"))
    placed = (
        P(PATH, FSDP, None),
        P(PATH, FSDP, None),
        P(None, PATH, None, FSDP),
        P(),
        P(),
        P(None, None, PATH, FSDP),
        P(None, None, PATH, FSDP),
    )
    return jax.shard_map(
        lambda *a: tuple(body(*a)),
        mesh=fine,
        in_specs=placed,
        out_specs=(P(None, None, PATH, FSDP), P(None, None, PATH, FSDP)),
        check_vma=False,
    )
```

```python
import functools

import jax
import jax.numpy as jnp
from jax import lax
from jax.experimental import pallas as pl
from jax.experimental.pallas import tpu as pltpu
from jax.sharding import Mesh, PartitionSpec as P

inner_step = 0.02
momentum_rate = 0.9
outer_rate = 0.7

CHIPS = ("zl", "y")
PATH = ("zl", "y", "core")
FSDP = ("zh", "x")
NX = 4
SHIFTS = (0, 2, 3, 1)
NZ = 4
LIMIT = 24 * 2**20
LARGE = 56 * 2**20
SMEM = pl.BlockSpec(memory_space=pltpu.SMEM)
VMEM = pl.BlockSpec(memory_space=pltpu.VMEM)
HBM = pl.BlockSpec(memory_space=pltpu.HBM)


def shift(axis, size, by):
    return [(i, (i + by) % size) for i in range(size)]


def params(limit=LIMIT):
    return pltpu.CompilerParams(vmem_limit_bytes=limit)


def pieces_to(where, shift_x, cot, hid, out):
    width = cot.shape[2]
    cols = hid.shape[2] // (NX * NZ)
    to = (where[1] + shift_x) % NX
    pairs = [(cot.at[0], out.at[:, pl.ds(0, width)])]
    for j in range(NZ):
        z = (where[0] + j) % NZ
        start = pl.multiple_of((z * NX + to) * cols, cols)
        pairs.append((hid.at[0, :, pl.ds(start, cols)], out.at[:, pl.ds(width + j * cols, cols)]))
    return pairs


def copy_all(pairs, sems):
    copies = [pltpu.make_async_copy(a, b, sems.at[i]) for i, (a, b) in enumerate(pairs)]
    for copy in copies:
        copy.start()
    for copy in copies:
        copy.wait()


def pack_kernel(cot, hid, *refs):
    *outs, packed = refs
    packed[...] = jnp.zeros_like(packed)
    zh, x = lax.axis_index("zh"), lax.axis_index("x")
    width = cot.shape[2]
    cols = hid.shape[2] // (NX * NZ)
    for k, out in enumerate(outs):
        to = (x + k + 1) % NX
        out[:, :width] = cot[0]
        for j in range(NZ):
            z = (zh + j) % NZ
            start = pl.multiple_of((z * NX + to) * cols, cols)
            out[:, width + j * cols : width + (j + 1) * cols] = hid[0, :, pl.ds(start, cols)]


def local_kernel(where, cot, hid, _, own, sems):
    copy_all(pieces_to(where, 0, cot, hid, own), sems)


def copy_kernel(source, _, out):
    out[...] = source[0, 0]


def masked_product(where, pieces, at, block, first, last):
    rows = pieces[0].shape[0]
    left = []
    for by, piece in zip(SHIFTS, pieces):
        source = (where[1] - by + NX) % NX
        token = (where[0] * NX + source) * rows + lax.broadcasted_iota(jnp.int32, (rows, block), 0)
        value = piece[:, pl.ds(at, block)].astype(jnp.float32)
        left.append(jnp.where(token < where[2], value, 0.0).astype(jnp.bfloat16))
    return inner_step * lax.dot_general(
        jnp.concatenate(left, axis=0),
        jnp.concatenate([piece[:, first:last] for piece in pieces], axis=0),
        (((0,), (0,)), ((), ())),
        preferred_element_type=jnp.float32,
    )


def grad_kernel(where, *refs):
    *pieces, drift, foreign, own = refs
    block, cols = own.shape
    at = pl.multiple_of(pl.program_id(0) * block, block)
    last = pieces[0].shape[1]
    part = masked_product(where, pieces, at, block, last - NZ * cols, last)
    own[...] = (part[:, :cols] + drift[0, 0].astype(jnp.float32)).astype(own.dtype)
    foreign[...] = part[:, cols:].astype(foreign.dtype)


def add_paths(weights, modules, level, got, total):
    def add(p, carry):
        m = modules[level, p]
        total[m] = total[m] + weights[level, p] * got[p].astype(jnp.float32)
        return carry

    lax.fori_loop(0, got.shape[0], add, 0, unroll=4)


def module_kernel(weights, modules, got, *refs):
    *outs, total = refs
    cols = outs[0].shape[2]
    total[...] = jnp.zeros_like(total)
    add_paths(weights, modules, 1, got, total)
    for k, out in enumerate(outs):
        out[...] = total[:, :, k * cols : (k + 1) * cols].astype(out.dtype)


def level0_kernel(where, weights, modules, got, mine, other, total):
    core, rows = where[2], mine.shape[1]
    total[...] = jnp.zeros_like(total)

    def add(i, carry):
        p = 2 * i + core
        m = modules[0, p]
        total[m] = total[m] + weights[0, p] * got[i].astype(jnp.float32)
        return carry

    lax.fori_loop(0, got.shape[0], add, 0, unroll=4)
    mine[...] = total[:, pl.ds(pl.multiple_of(core * rows, rows), rows)]
    other[...] = total[:, pl.ds(pl.multiple_of((1 - core) * rows, rows), rows)]


def update_kernel(weights, modules, mine0, other0, got, *refs):
    *parts, outer_params, outer_moment, new_params, new_moment, total = refs
    total[...] = functools.reduce(lambda a, b: a + b, [part[...].astype(jnp.float32) for part in parts])
    add_paths(weights, modules, 1, got, total)
    for level, average in ((0, mine0[...] + other0[...]), (1, total[...])):
        moment = momentum_rate * outer_moment[level] + average
        new_moment[level] = moment
        new_params[level] = outer_params[level] - outer_rate * (average + momentum_rate * moment)


def body(cotangent, hidden, drift, counts, assignment, outer_params, outer_moment):
    path_index = lax.axis_index(PATH)
    zh = lax.axis_index("zh")
    x = lax.axis_index("x")
    paths = counts.shape[0]
    modules = outer_params.shape[1]
    owner_rows = outer_params.shape[2]
    cols = outer_params.shape[3]
    rows = cotangent.shape[1]
    width = cotangent.shape[2]
    packed_shape = (rows, width + NZ * cols)
    foreign_cols = (NZ - 1) * cols
    bf16, f32 = jnp.bfloat16, jnp.float32

    place = jnp.stack([zh, x, lax.axis_index("core")]).astype(jnp.int32)
    step = 32
    *packed, after = pl.pallas_call(
        pack_kernel,
        out_shape=[jax.ShapeDtypeStruct(packed_shape, bf16)] * (NX - 1) + [jax.ShapeDtypeStruct((8, 128), f32)],
        grid=(rows // step,),
        in_specs=[
            pl.BlockSpec((1, step, width), lambda r: (0, r, 0)),
            pl.BlockSpec((1, step, hidden.shape[2]), lambda r: (0, r, 0)),
        ],
        out_specs=[pl.BlockSpec((step, packed_shape[1]), lambda r: (r, 0))] * (NX - 1)
        + [pl.BlockSpec((8, 128), lambda r: (0, 0))],
        compiler_params=params(LARGE),
    )(cotangent, hidden)
    pieces = [lax.ppermute(packed[k - 1], "x", shift("x", NX, k)) for k in SHIFTS[1:]]
    send0 = pl.pallas_call(
        copy_kernel,
        out_shape=jax.ShapeDtypeStruct((width, cols), bf16),
        grid=(1,),
        in_specs=[pl.BlockSpec((1, 1, width, cols), lambda r: (0, 0, 0, 0)), HBM],
        out_specs=pl.BlockSpec((width, cols), lambda r: (0, 0)),
        compiler_params=params(),
    )(drift, after)
    piece0 = pl.pallas_call(
        local_kernel,
        out_shape=jax.ShapeDtypeStruct(packed_shape, bf16),
        in_specs=[SMEM, HBM, HBM, HBM],
        out_specs=VMEM,
        scratch_shapes=[pltpu.SemaphoreType.DMA((1 + NZ,))],
        compiler_params=params(LARGE),
    )(place, cotangent, hidden, send0)
    pieces = [piece0] + pieces
    chips = paths // 2
    got0 = lax.all_to_all(
        send0.reshape(chips, 2 * owner_rows, cols), CHIPS, split_axis=0, concat_axis=0, tiled=True
    )

    member = (assignment[:, None, :] == jnp.arange(modules, dtype=jnp.int32)[None, :, None]).astype(f32)
    weighted = member * counts[None, None, :].astype(f32)
    shares = weighted / jnp.sum(weighted, axis=-1, keepdims=True)
    weights = jnp.sum(shares, axis=1)
    my_count = jnp.sum(jnp.where(jnp.arange(paths, dtype=jnp.int32) == path_index, counts, 0))
    where = jnp.stack([zh, x, my_count]).astype(jnp.int32)

    block = 256
    foreign, own = pl.pallas_call(
        grad_kernel,
        out_shape=[
            jax.ShapeDtypeStruct((width, foreign_cols), bf16),
            jax.ShapeDtypeStruct((width, cols), bf16),
        ],
        grid=(width // block,),
        in_specs=[SMEM] + [VMEM] * NX + [pl.BlockSpec((1, 1, block, cols), lambda r: (1, 0, r, 0))],
        out_specs=[
            pl.BlockSpec((block, foreign_cols), lambda r: (r, 0)),
            pl.BlockSpec((block, cols), lambda r: (r, 0)),
        ],
        compiler_params=params(),
        cost_estimate=pl.CostEstimate(flops=30 * 10**9, bytes_accessed=4 * 10**6, transcendentals=0),
    )(where, *pieces, drift)
    foreign, got0 = lax.optimization_barrier((foreign, got0))
    got_foreign = lax.all_to_all(
        foreign.reshape(paths, owner_rows, foreign_cols), PATH, split_axis=0, concat_axis=0, tiled=True
    )
    mine0, other0 = pl.pallas_call(
        level0_kernel,
        out_shape=[jax.ShapeDtypeStruct((modules, owner_rows, cols), f32)] * 2,
        in_specs=[SMEM, SMEM, SMEM, VMEM],
        out_specs=[VMEM, VMEM],
        scratch_shapes=[pltpu.VMEM((modules, 2 * owner_rows, cols), f32)],
        compiler_params=params(),
    )(place, weights, assignment, got0)
    other0 = lax.ppermute(other0, "core", shift("core", 2, 1))
    own, other0 = lax.optimization_barrier((own, other0))
    got_own = lax.all_to_all(
        own.reshape(paths, owner_rows, cols), PATH, split_axis=0, concat_axis=0, tiled=True
    )
    sums = pl.pallas_call(
        module_kernel,
        out_shape=[jax.ShapeDtypeStruct((modules, owner_rows, cols), bf16)] * (NZ - 1),
        in_specs=[SMEM, SMEM, VMEM],
        out_specs=[VMEM] * (NZ - 1),
        scratch_shapes=[pltpu.VMEM((modules, owner_rows, foreign_cols), f32)],
        compiler_params=params(),
    )(weights, assignment, got_foreign)
    parts = [lax.ppermute(sums[k - 1], "zh", shift("zh", NZ, k)) for k in SHIFTS[1:]]
    return pl.pallas_call(
        update_kernel,
        out_shape=[jax.ShapeDtypeStruct(outer_params.shape, f32)] * 2,
        in_specs=[SMEM, SMEM] + [VMEM] * (NZ + 4),
        out_specs=[VMEM] * 2,
        scratch_shapes=[pltpu.VMEM((modules, owner_rows, cols), f32)],
        compiler_params=params(),
    )(weights, assignment, mine0, other0, got_own, *parts, outer_params, outer_moment)


def solution(mesh):
    fine = Mesh(mesh.devices.reshape(4, 8, 2, 4, 4), ("zl", "y", "core", "zh", "x"))
    placed = (
        P(PATH, FSDP, None),
        P(PATH, FSDP, None),
        P(None, PATH, None, FSDP),
        P(),
        P(),
        P(None, None, PATH, FSDP),
        P(None, None, PATH, FSDP),
    )
    return jax.shard_map(
        lambda *a: tuple(body(*a)),
        mesh=fine,
        in_specs=placed,
        out_specs=(P(None, None, PATH, FSDP), P(None, None, PATH, FSDP)),
        check_vma=False,
    )
```

```python
import functools

import jax
import jax.numpy as jnp
from jax import lax
from jax.experimental import pallas as pl
from jax.experimental.pallas import tpu as pltpu
from jax.sharding import Mesh, PartitionSpec as P

inner_step = 0.02
momentum_rate = 0.9
outer_rate = 0.7

CHIPS = ("zl", "y")
PATH = ("zl", "y", "core")
FSDP = ("zh", "x")
NX = 4
SHIFTS = (0, 2, 3, 1)
NZ = 4
LIMIT = 24 * 2**20
LARGE = 56 * 2**20
SMEM = pl.BlockSpec(memory_space=pltpu.SMEM)
VMEM = pl.BlockSpec(memory_space=pltpu.VMEM)
HBM = pl.BlockSpec(memory_space=pltpu.HBM)


def shift(axis, size, by):
    return [(i, (i + by) % size) for i in range(size)]


def params(limit=LIMIT):
    return pltpu.CompilerParams(vmem_limit_bytes=limit)


def pieces_to(where, shift_x, cot, hid, out):
    width = cot.shape[2]
    cols = hid.shape[2] // (NX * NZ)
    to = (where[1] + shift_x) % NX
    pairs = [(cot.at[0], out.at[:, pl.ds(0, width)])]
    for j in range(NZ):
        z = (where[0] + j) % NZ
        start = pl.multiple_of((z * NX + to) * cols, cols)
        pairs.append((hid.at[0, :, pl.ds(start, cols)], out.at[:, pl.ds(width + j * cols, cols)]))
    return pairs


def copy_all(pairs, sems):
    copies = [pltpu.make_async_copy(a, b, sems.at[i]) for i, (a, b) in enumerate(pairs)]
    for copy in copies:
        copy.start()
    for copy in copies:
        copy.wait()


def pack_kernel(cot, hid, drift, *refs):
    *outs, send0 = refs
    send0[...] = drift[0, 0]
    zh, x = lax.axis_index("zh"), lax.axis_index("x")
    width = cot.shape[2]
    cols = hid.shape[2] // (NX * NZ)
    for k, out in enumerate(outs):
        to = (x + k + 1) % NX
        out[:, :width] = cot[0]
        for j in range(NZ):
            z = (zh + j) % NZ
            start = pl.multiple_of((z * NX + to) * cols, cols)
            out[:, width + j * cols : width + (j + 1) * cols] = hid[0, :, pl.ds(start, cols)]


def local_kernel(where, cot, hid, _, own, sems):
    copy_all(pieces_to(where, 0, cot, hid, own), sems)


def masked_product(where, pieces, at, block, first, last):
    rows = pieces[0].shape[0]
    left = []
    for by, piece in zip(SHIFTS, pieces):
        source = (where[1] - by + NX) % NX
        token = (where[0] * NX + source) * rows + lax.broadcasted_iota(jnp.int32, (rows, block), 0)
        value = piece[:, pl.ds(at, block)].astype(jnp.float32)
        left.append(jnp.where(token < where[2], value, 0.0).astype(jnp.bfloat16))
    return inner_step * lax.dot_general(
        jnp.concatenate(left, axis=0),
        jnp.concatenate([piece[:, first:last] for piece in pieces], axis=0),
        (((0,), (0,)), ((), ())),
        preferred_element_type=jnp.float32,
    )


def grad_kernel(where, *refs):
    *pieces, drift, foreign, own = refs
    block, cols = own.shape
    at = pl.multiple_of(pl.program_id(0) * block, block)
    last = pieces[0].shape[1]
    part = masked_product(where, pieces, at, block, last - NZ * cols, last)
    own[...] = (part[:, :cols] + drift[0, 0].astype(jnp.float32)).astype(own.dtype)
    foreign[...] = part[:, cols:].astype(foreign.dtype)


def add_paths(weights, modules, level, got, total):
    def add(p, carry):
        m = modules[level, p]
        total[m] = total[m] + weights[level, p] * got[p].astype(jnp.float32)
        return carry

    lax.fori_loop(0, got.shape[0], add, 0, unroll=4)


def module_kernel(weights, modules, got, *refs):
    *outs, total = refs
    cols = outs[0].shape[2]
    total[...] = jnp.zeros_like(total)
    add_paths(weights, modules, 1, got, total)
    for k, out in enumerate(outs):
        out[...] = total[:, :, k * cols : (k + 1) * cols].astype(out.dtype)


def level0_kernel(where, weights, modules, got, mine, other, total):
    core, rows = where[2], mine.shape[1]
    total[...] = jnp.zeros_like(total)

    def add(i, carry):
        p = 2 * i + core
        m = modules[0, p]
        total[m] = total[m] + weights[0, p] * got[i].astype(jnp.float32)
        return carry

    lax.fori_loop(0, got.shape[0], add, 0, unroll=4)
    mine[...] = total[:, pl.ds(pl.multiple_of(core * rows, rows), rows)]
    other[...] = total[:, pl.ds(pl.multiple_of((1 - core) * rows, rows), rows)]


def update_kernel(weights, modules, mine0, other0, got, *refs):
    *parts, outer_params, outer_moment, new_params, new_moment, total = refs
    total[...] = functools.reduce(lambda a, b: a + b, [part[...].astype(jnp.float32) for part in parts])
    add_paths(weights, modules, 1, got, total)
    for level, average in ((0, mine0[...] + other0[...]), (1, total[...])):
        moment = momentum_rate * outer_moment[level] + average
        new_moment[level] = moment
        new_params[level] = outer_params[level] - outer_rate * (average + momentum_rate * moment)


def body(cotangent, hidden, drift, counts, assignment, outer_params, outer_moment):
    path_index = lax.axis_index(PATH)
    zh = lax.axis_index("zh")
    x = lax.axis_index("x")
    paths = counts.shape[0]
    modules = outer_params.shape[1]
    owner_rows = outer_params.shape[2]
    cols = outer_params.shape[3]
    rows = cotangent.shape[1]
    width = cotangent.shape[2]
    packed_shape = (rows, width + NZ * cols)
    foreign_cols = (NZ - 1) * cols
    bf16, f32 = jnp.bfloat16, jnp.float32

    place = jnp.stack([zh, x, lax.axis_index("core")]).astype(jnp.int32)
    step = 64
    part = width // (rows // step)
    *packed, send0 = pl.pallas_call(
        pack_kernel,
        out_shape=[jax.ShapeDtypeStruct(packed_shape, bf16)] * (NX - 1)
        + [jax.ShapeDtypeStruct((width, cols), bf16)],
        grid=(rows // step,),
        in_specs=[
            pl.BlockSpec((1, step, width), lambda r: (0, r, 0)),
            pl.BlockSpec((1, step, hidden.shape[2]), lambda r: (0, r, 0)),
            pl.BlockSpec((1, 1, part, cols), lambda r: (0, 0, r, 0)),
        ],
        out_specs=[pl.BlockSpec((step, packed_shape[1]), lambda r: (r, 0))] * (NX - 1)
        + [pl.BlockSpec((part, cols), lambda r: (r, 0))],
        compiler_params=params(LARGE),
    )(cotangent, hidden, drift)
    pieces = [lax.ppermute(packed[k - 1], "x", shift("x", NX, k)) for k in SHIFTS[1:]]
    piece0 = pl.pallas_call(
        local_kernel,
        out_shape=jax.ShapeDtypeStruct(packed_shape, bf16),
        in_specs=[SMEM, HBM, HBM, HBM],
        out_specs=VMEM,
        scratch_shapes=[pltpu.SemaphoreType.DMA((1 + NZ,))],
        compiler_params=params(LARGE),
    )(place, cotangent, hidden, send0)
    pieces = [piece0] + pieces
    chips = paths // 2
    got0 = lax.all_to_all(
        send0.reshape(chips, 2 * owner_rows, cols), CHIPS, split_axis=0, concat_axis=0, tiled=True
    )

    member = (assignment[:, None, :] == jnp.arange(modules, dtype=jnp.int32)[None, :, None]).astype(f32)
    weighted = member * counts[None, None, :].astype(f32)
    shares = weighted / jnp.sum(weighted, axis=-1, keepdims=True)
    weights = jnp.sum(shares, axis=1)
    my_count = jnp.sum(jnp.where(jnp.arange(paths, dtype=jnp.int32) == path_index, counts, 0))
    where = jnp.stack([zh, x, my_count]).astype(jnp.int32)

    block = 256
    foreign, own = pl.pallas_call(
        grad_kernel,
        out_shape=[
            jax.ShapeDtypeStruct((width, foreign_cols), bf16),
            jax.ShapeDtypeStruct((width, cols), bf16),
        ],
        grid=(width // block,),
        in_specs=[SMEM] + [VMEM] * NX + [pl.BlockSpec((1, 1, block, cols), lambda r: (1, 0, r, 0))],
        out_specs=[
            pl.BlockSpec((block, foreign_cols), lambda r: (r, 0)),
            pl.BlockSpec((block, cols), lambda r: (r, 0)),
        ],
        compiler_params=params(),
        cost_estimate=pl.CostEstimate(flops=30 * 10**9, bytes_accessed=4 * 10**6, transcendentals=0),
    )(where, *pieces, drift)
    foreign, got0 = lax.optimization_barrier((foreign, got0))
    got_foreign = lax.all_to_all(
        foreign.reshape(paths, owner_rows, foreign_cols), PATH, split_axis=0, concat_axis=0, tiled=True
    )
    mine0, other0 = pl.pallas_call(
        level0_kernel,
        out_shape=[jax.ShapeDtypeStruct((modules, owner_rows, cols), f32)] * 2,
        in_specs=[SMEM, SMEM, SMEM, VMEM],
        out_specs=[VMEM, VMEM],
        scratch_shapes=[pltpu.VMEM((modules, 2 * owner_rows, cols), f32)],
        compiler_params=params(),
    )(place, weights, assignment, got0)
    other0 = lax.ppermute(other0, "core", shift("core", 2, 1))
    own, other0 = lax.optimization_barrier((own, other0))
    got_own = lax.all_to_all(
        own.reshape(paths, owner_rows, cols), PATH, split_axis=0, concat_axis=0, tiled=True
    )
    sums = pl.pallas_call(
        module_kernel,
        out_shape=[jax.ShapeDtypeStruct((modules, owner_rows, cols), bf16)] * (NZ - 1),
        in_specs=[SMEM, SMEM, VMEM],
        out_specs=[VMEM] * (NZ - 1),
        scratch_shapes=[pltpu.VMEM((modules, owner_rows, foreign_cols), f32)],
        compiler_params=params(),
    )(weights, assignment, got_foreign)
    parts = [lax.ppermute(sums[k - 1], "zh", shift("zh", NZ, k)) for k in SHIFTS[1:]]
    return pl.pallas_call(
        update_kernel,
        out_shape=[jax.ShapeDtypeStruct(outer_params.shape, f32)] * 2,
        in_specs=[SMEM, SMEM] + [VMEM] * (NZ + 4),
        out_specs=[VMEM] * 2,
        scratch_shapes=[pltpu.VMEM((modules, owner_rows, cols), f32)],
        compiler_params=params(),
    )(weights, assignment, mine0, other0, got_own, *parts, outer_params, outer_moment)


def solution(mesh):
    fine = Mesh(mesh.devices.reshape(4, 8, 2, 4, 4), ("zl", "y", "core", "zh", "x"))
    placed = (
        P(PATH, FSDP, None),
        P(PATH, FSDP, None),
        P(None, PATH, None, FSDP),
        P(),
        P(),
        P(None, None, PATH, FSDP),
        P(None, None, PATH, FSDP),
    )
    return jax.shard_map(
        lambda *a: tuple(body(*a)),
        mesh=fine,
        in_specs=placed,
        out_specs=(P(None, None, PATH, FSDP), P(None, None, PATH, FSDP)),
        check_vma=False,
    )
```

```python
import functools

import jax
import jax.numpy as jnp
from jax import lax
from jax.experimental import pallas as pl
from jax.experimental.pallas import tpu as pltpu
from jax.sharding import Mesh, PartitionSpec as P

inner_step = 0.02
momentum_rate = 0.9
outer_rate = 0.7

CHIPS = ("zl", "y")
PATH = ("zl", "y", "core")
FSDP = ("zh", "x")
NX = 4
SHIFTS = (0, 2, 3, 1)
NZ = 4
LIMIT = 24 * 2**20
LARGE = 56 * 2**20
SMEM = pl.BlockSpec(memory_space=pltpu.SMEM)
VMEM = pl.BlockSpec(memory_space=pltpu.VMEM)
HBM = pl.BlockSpec(memory_space=pltpu.HBM)


def shift(axis, size, by):
    return [(i, (i + by) % size) for i in range(size)]


def params(limit=LIMIT):
    return pltpu.CompilerParams(vmem_limit_bytes=limit)


def pieces_to(where, shift_x, cot, hid, out):
    width = cot.shape[2]
    cols = hid.shape[2] // (NX * NZ)
    to = (where[1] + shift_x) % NX
    pairs = [(cot.at[0], out.at[:, pl.ds(0, width)])]
    for j in range(NZ):
        z = (where[0] + j) % NZ
        start = pl.multiple_of((z * NX + to) * cols, cols)
        pairs.append((hid.at[0, :, pl.ds(start, cols)], out.at[:, pl.ds(width + j * cols, cols)]))
    return pairs


def copy_all(pairs, sems):
    copies = [pltpu.make_async_copy(a, b, sems.at[i]) for i, (a, b) in enumerate(pairs)]
    for copy in copies:
        copy.start()
    for copy in copies:
        copy.wait()


def pack_kernel(cot, hid, drift, *refs):
    *outs, send0 = refs
    send0[...] = drift[0, 0]
    zh, x = lax.axis_index("zh"), lax.axis_index("x")
    width = cot.shape[2]
    cols = hid.shape[2] // (NX * NZ)
    for k, out in enumerate(outs):
        to = (x + k + 1) % NX
        out[:, :width] = cot[0]
        for j in range(NZ):
            z = (zh + j) % NZ
            start = pl.multiple_of((z * NX + to) * cols, cols)
            out[:, width + j * cols : width + (j + 1) * cols] = hid[0, :, pl.ds(start, cols)]


def local_kernel(where, cot, hid, _, own, sems):
    copy_all(pieces_to(where, 0, cot, hid, own), sems)


def masked_product(where, pieces, at, block, first, last):
    rows = pieces[0].shape[0]
    left = []
    for by, piece in zip(SHIFTS, pieces):
        source = (where[1] - by + NX) % NX
        token = (where[0] * NX + source) * rows + lax.broadcasted_iota(jnp.int32, (rows, block), 0)
        value = piece[:, pl.ds(at, block)].astype(jnp.float32)
        left.append(jnp.where(token < where[2], value, 0.0).astype(jnp.bfloat16))
    return inner_step * lax.dot_general(
        jnp.concatenate(left, axis=0),
        jnp.concatenate([piece[:, first:last] for piece in pieces], axis=0),
        (((0,), (0,)), ((), ())),
        preferred_element_type=jnp.float32,
    )


def grad_kernel(where, *refs):
    *pieces, drift, foreign, own = refs
    block, cols = own.shape
    at = pl.multiple_of(pl.program_id(0) * block, block)
    last = pieces[0].shape[1]
    part = masked_product(where, pieces, at, block, last - NZ * cols, last)
    own[...] = (part[:, :cols] + drift[0, 0].astype(jnp.float32)).astype(own.dtype)
    foreign[...] = part[:, cols:].astype(foreign.dtype)


def add_paths(weights, modules, level, got, total):
    def add(p, carry):
        m = modules[level, p]
        total[m] = total[m] + weights[level, p] * got[p].astype(jnp.float32)
        return carry

    lax.fori_loop(0, got.shape[0], add, 0, unroll=16)


def module_kernel(weights, modules, got, *refs):
    *outs, total = refs
    cols = outs[0].shape[2]
    total[...] = jnp.zeros_like(total)
    add_paths(weights, modules, 1, got, total)
    for k, out in enumerate(outs):
        out[...] = total[:, :, k * cols : (k + 1) * cols].astype(out.dtype)


def level0_kernel(where, weights, modules, got, mine, other, total):
    core, rows = where[2], mine.shape[1]
    total[...] = jnp.zeros_like(total)

    def add(i, carry):
        p = 2 * i + core
        m = modules[0, p]
        total[m] = total[m] + weights[0, p] * got[i].astype(jnp.float32)
        return carry

    lax.fori_loop(0, got.shape[0], add, 0, unroll=16)
    mine[...] = total[:, pl.ds(pl.multiple_of(core * rows, rows), rows)]
    other[...] = total[:, pl.ds(pl.multiple_of((1 - core) * rows, rows), rows)]


def update_kernel(weights, modules, mine0, other0, got, *refs):
    *parts, outer_params, outer_moment, new_params, new_moment, total = refs
    total[...] = functools.reduce(lambda a, b: a + b, [part[...].astype(jnp.float32) for part in parts])
    add_paths(weights, modules, 1, got, total)
    for level, average in ((0, mine0[...] + other0[...]), (1, total[...])):
        moment = momentum_rate * outer_moment[level] + average
        new_moment[level] = moment
        new_params[level] = outer_params[level] - outer_rate * (average + momentum_rate * moment)


def body(cotangent, hidden, drift, counts, assignment, outer_params, outer_moment):
    path_index = lax.axis_index(PATH)
    zh = lax.axis_index("zh")
    x = lax.axis_index("x")
    paths = counts.shape[0]
    modules = outer_params.shape[1]
    owner_rows = outer_params.shape[2]
    cols = outer_params.shape[3]
    rows = cotangent.shape[1]
    width = cotangent.shape[2]
    packed_shape = (rows, width + NZ * cols)
    foreign_cols = (NZ - 1) * cols
    bf16, f32 = jnp.bfloat16, jnp.float32

    place = jnp.stack([zh, x, lax.axis_index("core")]).astype(jnp.int32)
    step = 64
    part = width // (rows // step)
    *packed, send0 = pl.pallas_call(
        pack_kernel,
        out_shape=[jax.ShapeDtypeStruct(packed_shape, bf16)] * (NX - 1)
        + [jax.ShapeDtypeStruct((width, cols), bf16)],
        grid=(rows // step,),
        in_specs=[
            pl.BlockSpec((1, step, width), lambda r: (0, r, 0)),
            pl.BlockSpec((1, step, hidden.shape[2]), lambda r: (0, r, 0)),
            pl.BlockSpec((1, 1, part, cols), lambda r: (0, 0, r, 0)),
        ],
        out_specs=[pl.BlockSpec((step, packed_shape[1]), lambda r: (r, 0))] * (NX - 1)
        + [pl.BlockSpec((part, cols), lambda r: (r, 0))],
        compiler_params=params(LARGE),
    )(cotangent, hidden, drift)
    pieces = [lax.ppermute(packed[k - 1], "x", shift("x", NX, k)) for k in SHIFTS[1:]]
    piece0 = pl.pallas_call(
        local_kernel,
        out_shape=jax.ShapeDtypeStruct(packed_shape, bf16),
        in_specs=[SMEM, HBM, HBM, HBM],
        out_specs=VMEM,
        scratch_shapes=[pltpu.SemaphoreType.DMA((1 + NZ,))],
        compiler_params=params(LARGE),
    )(place, cotangent, hidden, send0)
    pieces = [piece0] + pieces
    chips = paths // 2
    got0 = lax.all_to_all(
        send0.reshape(chips, 2 * owner_rows, cols), CHIPS, split_axis=0, concat_axis=0, tiled=True
    )

    member = (assignment[:, None, :] == jnp.arange(modules, dtype=jnp.int32)[None, :, None]).astype(f32)
    weighted = member * counts[None, None, :].astype(f32)
    shares = weighted / jnp.sum(weighted, axis=-1, keepdims=True)
    weights = jnp.sum(shares, axis=1)
    my_count = jnp.sum(jnp.where(jnp.arange(paths, dtype=jnp.int32) == path_index, counts, 0))
    where = jnp.stack([zh, x, my_count]).astype(jnp.int32)

    block = 256
    foreign, own = pl.pallas_call(
        grad_kernel,
        out_shape=[
            jax.ShapeDtypeStruct((width, foreign_cols), bf16),
            jax.ShapeDtypeStruct((width, cols), bf16),
        ],
        grid=(width // block,),
        in_specs=[SMEM] + [VMEM] * NX + [pl.BlockSpec((1, 1, block, cols), lambda r: (1, 0, r, 0))],
        out_specs=[
            pl.BlockSpec((block, foreign_cols), lambda r: (r, 0)),
            pl.BlockSpec((block, cols), lambda r: (r, 0)),
        ],
        compiler_params=params(),
        cost_estimate=pl.CostEstimate(flops=30 * 10**9, bytes_accessed=4 * 10**6, transcendentals=0),
    )(where, *pieces, drift)
    foreign, got0 = lax.optimization_barrier((foreign, got0))
    got_foreign = lax.all_to_all(
        foreign.reshape(paths, owner_rows, foreign_cols), PATH, split_axis=0, concat_axis=0, tiled=True
    )
    mine0, other0 = pl.pallas_call(
        level0_kernel,
        out_shape=[jax.ShapeDtypeStruct((modules, owner_rows, cols), f32)] * 2,
        in_specs=[SMEM, SMEM, SMEM, VMEM],
        out_specs=[VMEM, VMEM],
        scratch_shapes=[pltpu.VMEM((modules, 2 * owner_rows, cols), f32)],
        compiler_params=params(),
    )(place, weights, assignment, got0)
    other0 = lax.ppermute(other0, "core", shift("core", 2, 1))
    own, other0 = lax.optimization_barrier((own, other0))
    got_own = lax.all_to_all(
        own.reshape(paths, owner_rows, cols), PATH, split_axis=0, concat_axis=0, tiled=True
    )
    sums = pl.pallas_call(
        module_kernel,
        out_shape=[jax.ShapeDtypeStruct((modules, owner_rows, cols), bf16)] * (NZ - 1),
        in_specs=[SMEM, SMEM, VMEM],
        out_specs=[VMEM] * (NZ - 1),
        scratch_shapes=[pltpu.VMEM((modules, owner_rows, foreign_cols), f32)],
        compiler_params=params(),
    )(weights, assignment, got_foreign)
    parts = [lax.ppermute(sums[k - 1], "zh", shift("zh", NZ, k)) for k in SHIFTS[1:]]
    return pl.pallas_call(
        update_kernel,
        out_shape=[jax.ShapeDtypeStruct(outer_params.shape, f32)] * 2,
        in_specs=[SMEM, SMEM] + [VMEM] * (NZ + 4),
        out_specs=[VMEM] * 2,
        scratch_shapes=[pltpu.VMEM((modules, owner_rows, cols), f32)],
        compiler_params=params(),
    )(weights, assignment, mine0, other0, got_own, *parts, outer_params, outer_moment)


def solution(mesh):
    fine = Mesh(mesh.devices.reshape(4, 8, 2, 4, 4), ("zl", "y", "core", "zh", "x"))
    placed = (
        P(PATH, FSDP, None),
        P(PATH, FSDP, None),
        P(None, PATH, None, FSDP),
        P(),
        P(),
        P(None, None, PATH, FSDP),
        P(None, None, PATH, FSDP),
    )
    return jax.shard_map(
        lambda *a: tuple(body(*a)),
        mesh=fine,
        in_specs=placed,
        out_specs=(P(None, None, PATH, FSDP), P(None, None, PATH, FSDP)),
        check_vma=False,
    )
```
